1024 devices in a mesh: blk: 256 (over y_hi, z, x), grp: 4 (over y_lo, core).
Axes of the slice: x: 4, y: 4 (y_hi: 2, y_lo: 2; y = y_hi * 2 + y_lo), z: 32, core: 2. Of those that a mesh axis runs over, the one named last changes fastest.
Arguments:
- images: bfloat16 [131072, 1152], P(('blk', 'grp')), as said below
- texts: bfloat16 [131072, 1152], P(('blk', 'grp')), as said below
- log_scale: float32 [1], replicated, may hold values from 1.6 to 2.6
- bias: float32 [1], replicated, may hold values from -3 to -1
Outputs:
- row_loss: float32 [131072], P(('blk', 'grp'))
- image_grad: float32 [131072, 1152], P(('blk', 'grp'))
- text_grad: float32 [131072, 1152], P(('blk', 'grp'))
The draws below stay inside these ranges and needn't reach their ends.
Inputs may be any that keep to these rules, and one draw needn't show every extreme that they name: `images`: rows of image embeddings come with different norms. `texts`: rows of text embeddings come with different norms.
All inputs are finite; a program needn't handle non-finite values.
Results may differ from the reference program's by a relative error of at most 0.0054.
Values may be sent and summed in bfloat16 or wider, within the bound.
No kernel may reach another device: no remote copies, remote signals or barrier semaphores. Data moves between devices by JAX's collectives and lax.ppermute only.
A program may use at most 32 MiB of HBM per device.

```python
import math
import jax
import jax.numpy as jnp
from jax import lax

D = 1152
STEPS = 3
SPAN = 512
BATCH = 131072


def shared_base(key):
    return jnp.clip(jax.random.normal(key, (BATCH, D), jnp.float32), -4.0, 4.0)


def row_spread(key, lowest, highest):
    level = jax.random.uniform(key, (BATCH, 1), jnp.float32)
    return jnp.exp(math.log(lowest) + level * (math.log(highest) - math.log(lowest)))


def draw_images(key, part):
    base = shared_base(key)
    key = jax.random.fold_in(key, 11)
    spread = row_spread(key, 0.5, 5.0)
    return (base * spread / math.sqrt(D)).astype(jnp.bfloat16)


def draw_texts(key, part):
    base = shared_base(key)
    key = jax.random.fold_in(key, 23)
    noise = jnp.clip(jax.random.normal(jax.random.fold_in(key, 1), (BATCH, D), jnp.float32), -4.0, 4.0)
    spread = row_spread(jax.random.fold_in(key, 2), 0.5, 5.0)
    mixed = 0.6 * base + 0.8 * noise
    return (mixed * spread / math.sqrt(D)).astype(jnp.bfloat16)


def setup_inputs(seed: int = 0) -> dict:
    seeds = jax.random.split(jax.random.key(seed), 5)
    images = draw_images(jax.random.fold_in(seeds[4], 71), 0)
    texts = draw_texts(jax.random.fold_in(seeds[4], 71), 0)
    log_scale = jnp.clip(jax.random.uniform(seeds[2], (1,), jnp.float32, 1.6, 2.6), 1.6, 2.6)
    bias = jnp.clip(jax.random.uniform(seeds[3], (1,), jnp.float32, -3.0, -1.0), -3.0, -1.0)
    return {"images": images, "texts": texts, "log_scale": log_scale, "bias": bias}


def unit_rows(values):
    wide = values.astype(jnp.float32)
    inverse = lax.rsqrt(lax.optimization_barrier(jnp.sum(wide * wide, axis=-1, keepdims=True)) + 1e-06)
    return ((wide * inverse).astype(jnp.bfloat16), inverse)

def pair_tile(image_unit, text_unit, scale, offset, positive):
    logit = scale * jnp.dot(image_unit, text_unit.T, preferred_element_type=jnp.float32) + offset
    signs = 2.0 * positive - 1.0
    term = jax.nn.softplus(-signs * logit)
    coef = (-signs * jax.nn.sigmoid(-signs * logit) * scale / STEPS).astype(jnp.bfloat16)
    return (lax.optimization_barrier(jnp.sum(term, axis=1)), coef)

def reference(images, texts, log_scale, bias):
    scale = jnp.exp(log_scale[0])
    offset = bias[0]
    image_unit, image_inv = unit_rows(images)
    text_unit, unused = unit_rows(texts)
    groups = BATCH // SPAN
    image_blocks = image_unit.reshape(groups, SPAN, D)
    text_blocks = text_unit.reshape(groups, SPAN, D)
    diagonal = jnp.eye(SPAN, dtype=jnp.float32)
    nothing = jnp.zeros((SPAN, SPAN), jnp.float32)

    def per_group(index):
        mine = image_blocks[index]
        loss = jnp.zeros((SPAN,), jnp.float32)
        grad = jnp.zeros((SPAN, D), jnp.float32)
        parts = []
        for step in range(STEPS):
            other = text_blocks[(index - step) % groups]
            positive = diagonal if step == 0 else nothing
            row_terms, coef = pair_tile(mine, other, scale, offset, positive)
            loss = loss + row_terms
            grad = grad + jnp.dot(coef, other, preferred_element_type=jnp.float32)
            parts.append(jnp.dot(coef.T, mine, preferred_element_type=jnp.float32))
        return (loss, grad, jnp.stack(parts))
    loss, grad, parts = lax.map(per_group, jnp.arange(groups, dtype=jnp.int32))
    text_sum = jnp.zeros((groups, SPAN, D), jnp.float32)
    for step in range(STEPS):
        text_sum = text_sum + jnp.roll(parts[:, step], STEPS - 1 - step, axis=0)
    grad = grad.reshape(BATCH, D)
    unit_wide = image_unit.astype(jnp.float32)
    along = lax.optimization_barrier(jnp.sum(unit_wide * grad, axis=1, keepdims=True))
    image_grad = image_inv * (grad - unit_wide * along)
    row_loss = loss.reshape(BATCH) / (STEPS * SPAN)
    return (row_loss, image_grad, text_sum.reshape(BATCH, D))
```

```python
import jax
import jax.numpy as jnp
from jax import lax
from jax.experimental import pallas as pl
from jax.experimental.pallas import tpu as pltpu
from jax.sharding import PartitionSpec as P

STEPS = 3
LOSS_ROWS = 16
F32 = jnp.float32
BF16 = jnp.bfloat16


def passed_along(block, distance):
    count = lax.axis_size("blk")
    return lax.ppermute(block, "blk", [(i, (i + distance) % count) for i in range(count)])


def swapped(block, flip):
    return lax.ppermute(block, "grp", [(i, i ^ flip) for i in range(lax.axis_size("grp"))])


def unit_rows(values):
    wide = values.astype(F32)
    inverse = lax.rsqrt(jnp.sum(wide * wide, axis=-1, keepdims=True) + 1e-06)
    return ((wide * inverse).astype(BF16), inverse)


def pair_terms(text_unit, image_units, log_scale, bias, positive=None):
    dots = lax.dot_general(
        text_unit, image_units, (((1,), (1,)), ((), ())), preferred_element_type=F32
    )
    scale = jnp.exp(jnp.full((1, dots.shape[1]), log_scale, F32))
    logit = scale * dots + bias
    value = logit if positive is None else jnp.where(positive, -logit, logit)
    small = jnp.exp(-jnp.abs(value))
    term = jnp.maximum(value, 0.0) + jnp.log1p(small)
    share = jnp.where(value >= 0.0, 1.0, small) / (1.0 + small)
    coef = share * (scale / STEPS)
    if positive is not None:
        coef = jnp.where(positive, -coef, coef)
    return (jnp.sum(term, axis=0, keepdims=True), coef.astype(BF16))


def by_image(coef, text_unit):
    return lax.dot_general(
        coef, text_unit, (((0,), (0,)), ((), ())), preferred_element_type=F32
    )


def coded_loss(loss, width):
    high = loss.astype(BF16)
    low = (loss - high.astype(F32)).astype(BF16)
    rows = loss.shape[1]
    half = LOSS_ROWS // 2
    parts = [jnp.broadcast_to(part.astype(F32), (half, rows)) for part in (high, low)]
    filled = jnp.concatenate([jnp.concatenate(parts, axis=0), jnp.zeros((LOSS_ROWS, width - rows), F32)], axis=1)
    return filled.astype(BF16)


def decoded_loss(tail, rows):
    wide = tail.astype(F32)
    half = LOSS_ROWS // 2
    return wide[0:1, :rows] + wide[half : half + 1, :rows]


def own_kernel(log_scale, bias, own, core, across, diagonal, texts, units, unit_out, coef_out, loss_out, text_part):
    rows = own.shape[0]
    for place, block in enumerate((own, core, across, diagonal)):
        units[place * rows : (place + 1) * rows, :] = unit_rows(block[...])[0]
    text_unit = unit_rows(texts[...])[0]
    unit_out[...] = text_unit
    everything = units[...]
    shape = (rows, everything.shape[0])
    positive = lax.broadcasted_iota(jnp.int32, shape, 0) == lax.broadcasted_iota(jnp.int32, shape, 1)
    loss, coef = pair_terms(text_unit, everything, log_scale[0], bias[0], positive)
    coef_out[...] = coef
    loss_out[...] = loss
    text_part[...] = jnp.dot(coef, everything, preferred_element_type=F32).astype(BF16)


def band_kernel(log_scale, bias, units, text_unit, coef_own, loss_own, texts_one, texts_two, to_core, kept, kept_loss, part_one, part_two):
    rows = texts_one.shape[0]
    width = texts_one.shape[1]
    everything = units[...]
    one = unit_rows(texts_one[...])[0]
    two = unit_rows(texts_two[...])[0]
    loss_one, coef_one = pair_terms(one, everything, log_scale[0], bias[0])
    loss_two, coef_two = pair_terms(two, everything, log_scale[0], bias[0])
    part_one[...] = jnp.dot(coef_one, everything, preferred_element_type=F32).astype(BF16)
    part_two[...] = jnp.dot(coef_two, everything, preferred_element_type=F32)
    loss = loss_own[...] + loss_one + loss_two
    coef_zero = coef_own[...]
    unit_zero = text_unit[...]
    for place, (home, slot) in enumerate(((kept, 0), (to_core, 0), (kept, 1), (to_core, 1))):
        part = slice(place * rows, (place + 1) * rows)
        total = by_image(coef_zero[:, part], unit_zero) + by_image(coef_one[:, part], one) + by_image(coef_two[:, part], two)
        if home is kept:
            kept[slot] = total
            kept_loss[slot : slot + 1, :] = loss[:, part]
        else:
            to_core[slot, :rows, :] = total.astype(BF16)
            to_core[slot, rows:, :] = coded_loss(loss[:, part], width)


def pair_kernel(kept, kept_loss, from_core, to_across):
    rows = kept.shape[1]
    to_across[:rows, :] = (kept[1] + from_core[1, :rows, :].astype(F32)).astype(BF16)
    loss = kept_loss[1:2, :] + decoded_loss(from_core[1, rows:, :], rows)
    to_across[rows:, :] = coded_loss(loss, kept.shape[2])


def last_kernel(images, kept, kept_loss, from_core, from_across, image_grad, row_loss):
    rows = images.shape[0]
    unit, inverse = unit_rows(images[...])
    grad = kept[0] + from_core[0, :rows, :].astype(F32) + from_across[:rows, :].astype(F32)
    wide = unit.astype(F32)
    along = jnp.sum(wide * grad, axis=1, keepdims=True)
    image_grad[...] = inverse * (grad - wide * along)
    loss = kept_loss[0:1, :] + decoded_loss(from_core[0, rows:, :], rows) + decoded_loss(from_across[rows:, :], rows)
    row_loss[...] = loss / (STEPS * 4 * rows)


def call(kernel, name, outs, arguments, scalars=0, flops=0):
    in_specs = [pl.BlockSpec(memory_space=pltpu.SMEM)] * scalars
    in_specs += [pl.BlockSpec(memory_space=pltpu.VMEM)] * (len(arguments) - scalars)
    moved = sum(a.size * a.dtype.itemsize for a in (*arguments, *outs))
    return pl.pallas_call(
        kernel,
        name=name,
        out_shape=outs,
        in_specs=in_specs,
        out_specs=tuple(pl.BlockSpec(memory_space=pltpu.VMEM) for _ in outs),
        cost_estimate=pl.CostEstimate(flops=flops, bytes_accessed=moved, transcendentals=0),
        compiler_params=pltpu.CompilerParams(vmem_limit_bytes=24 * 1024 * 1024),
    )(*arguments)


def shards(images, texts, log_scale, bias):
    rows, width = images.shape
    span = rows * lax.axis_size("grp")
    tall = rows + LOSS_ROWS
    made = jax.ShapeDtypeStruct
    across = swapped(images, 2)
    texts_one = passed_along(texts, 1)
    texts_two = passed_along(texts, 2)
    core = swapped(images, 1)
    diagonal = swapped(across, 1)
    matmul = 2 * rows * span * width
    units, text_unit, coef, loss, part_zero = call(
        own_kernel,
        "own_texts",
        (
            made((span, width), BF16),
            made((rows, width), BF16),
            made((rows, span), BF16),
            made((1, span), F32),
            made((rows, width), BF16),
        ),
        (log_scale, bias, images, core, across, diagonal, texts),
        2,
        2 * matmul,
    )
    part_zero = passed_along(part_zero, 2)
    to_core, kept, kept_loss, part_one, part_two = call(
        band_kernel,
        "band_texts",
        (
            made((2, tall, width), BF16),
            made((2, rows, width), F32),
            made((2, rows), F32),
            made((rows, width), BF16),
            made((rows, width), F32),
        ),
        (log_scale, bias, units, text_unit, coef, loss, texts_one, texts_two),
        2,
        7 * matmul,
    )
    from_core = swapped(to_core, 1)
    part_one = passed_along(part_one, 1)
    (to_across,) = call(pair_kernel, "chip_sum", (made((tall, width), BF16),), (kept, kept_loss, from_core))
    from_across = swapped(to_across, 2)
    text_grad = part_two + part_one.astype(F32) + part_zero.astype(F32)
    image_grad, row_loss = call(
        last_kernel,
        "image_grad",
        (made((rows, width), F32), made((1, rows), F32)),
        (images, kept, kept_loss, from_core, from_across),
    )
    return (row_loss.reshape(rows), image_grad, text_grad)


def solution(mesh):
    return jax.shard_map(
        shards,
        mesh=mesh,
        in_specs=(P(("blk", "grp"), None), P(("blk", "grp"), None), P(), P()),
        out_specs=(P(("blk", "grp")), P(("blk", "grp"), None), P(("blk", "grp"), None)),
        check_vma=False,
    )
```

```python
import jax
import jax.numpy as jnp
from jax import lax
from jax.experimental import pallas as pl
from jax.experimental.pallas import tpu as pltpu
from jax.sharding import PartitionSpec as P

STEPS = 3
LOSS_ROWS = 16
F32 = jnp.float32
BF16 = jnp.bfloat16


def passed_along(block, flips):
    groups = lax.axis_size("blk")
    members = lax.axis_size("grp")
    route = []
    for group in range(groups):
        flip = 2 if group % (groups // 2) in flips else 0
        for member in range(members):
            target = (group + 1) % groups * members + (member ^ flip)
            route.append((group * members + member, target))
    return lax.ppermute(block, ("blk", "grp"), route)


def passed_two(block):
    groups = lax.axis_size("blk")
    return lax.ppermute(block, "blk", [(i, (i + 2) % groups) for i in range(groups)])


def swapped(block, flip):
    return lax.ppermute(block, "grp", [(i, i ^ flip) for i in range(lax.axis_size("grp"))])


def unit_rows(values):
    wide = values.astype(F32)
    inverse = lax.rsqrt(jnp.sum(wide * wide, axis=-1, keepdims=True) + 1e-06)
    return ((wide * inverse).astype(BF16), inverse)


def pair_terms(text_unit, image_units, scale, bias, positive=None):
    dots = lax.dot_general(
        text_unit, image_units, (((1,), (1,)), ((), ())), preferred_element_type=F32
    )
    logit = scale * dots + bias
    value = logit if positive is None else jnp.where(positive, -logit, logit)
    small = jnp.exp(-jnp.abs(value))
    term = jnp.maximum(value, 0.0) + jnp.log1p(small)
    share = jnp.where(value >= 0.0, 1.0, small) / (1.0 + small)
    coef = share * (scale / STEPS)
    if positive is not None:
        coef = jnp.where(positive, -coef, coef)
    return (jnp.sum(term, axis=0, keepdims=True), coef.astype(BF16))


def by_image(coef, text_unit):
    return lax.dot_general(
        coef, text_unit, (((0,), (0,)), ((), ())), preferred_element_type=F32
    )


def coded_loss(loss, width):
    high = loss.astype(BF16)
    low = (loss - high.astype(F32)).astype(BF16)
    rows = loss.shape[1]
    half = LOSS_ROWS // 2
    parts = [jnp.broadcast_to(part.astype(F32), (half, rows)) for part in (high, low)]
    filled = jnp.concatenate([jnp.concatenate(parts, axis=0), jnp.zeros((LOSS_ROWS, width - rows), F32)], axis=1)
    return filled.astype(BF16)


def decoded_loss(tail, rows):
    wide = tail.astype(F32)
    half = LOSS_ROWS // 2
    return wide[0:1, :rows] + wide[half : half + 1, :rows]


def own_kernel(log_scale, bias, images, texts, image_unit, text_unit, knobs, inverses):
    unit, inverse = unit_rows(images[...])
    image_unit[...] = unit
    inverses[...] = jnp.broadcast_to(inverse, inverses.shape)
    text_unit[...] = unit_rows(texts[...])[0]
    span = knobs.shape[1]
    knobs[0:1, :] = jnp.exp(jnp.full((1, span), log_scale[0], F32))
    knobs[1:2, :] = jnp.full((1, span), bias[0], F32)


def near_kernel(knobs, image_unit, text_unit, core, across, diagonal, texts_one, units, text_units, coefs, losses, part_zero, part_one):
    rows = image_unit.shape[0]
    units[:rows, :] = image_unit[...]
    for place, block in ((1, core), (2, across), (3, diagonal)):
        units[place * rows : (place + 1) * rows, :] = unit_rows(block[...])[0]
    scale, offset = knobs[0:1, :], knobs[1:2, :]
    everything = units[...]
    shape = (rows, everything.shape[0])
    positive = lax.broadcasted_iota(jnp.int32, shape, 0) == lax.broadcasted_iota(jnp.int32, shape, 1)
    total = None
    for step, part in enumerate((part_zero, part_one)):
        unit = text_unit[...] if step == 0 else unit_rows(texts_one[...])[0]
        loss, coef = pair_terms(unit, everything, scale, offset, positive if step == 0 else None)
        text_units[step * rows : (step + 1) * rows, :] = unit
        coefs[step * rows : (step + 1) * rows, :] = coef
        part[...] = jnp.dot(coef, everything, preferred_element_type=F32).astype(BF16)
        total = loss if total is None else total + loss
    losses[...] = total


def image_part(coefs, text_units, coef_two, unit_two, place):
    rows = unit_two.shape[0]
    part = slice(place * rows, (place + 1) * rows)
    return by_image(coefs[:, part], text_units[...]) + by_image(coef_two[:, part], unit_two)


def far_kernel(knobs, units, text_units, coefs, losses, texts_two, coef_out, unit_out, loss_out, to_core_top, to_core_low):
    rows, width = texts_two.shape
    unit_two = unit_rows(texts_two[...])[0]
    loss, coef = pair_terms(unit_two, units[...], knobs[0:1, :], knobs[1:2, :])
    unit_out[...] = unit_two
    coef_out[...] = coef
    loss = losses[...] + loss
    loss_out[...] = loss
    part = image_part(coefs, text_units, coef, unit_two, 3).astype(BF16)
    half = rows // 2
    to_core_top[...] = part[:half]
    to_core_low[:half, :] = part[half:]
    to_core_low[half : half + LOSS_ROWS, :] = coded_loss(loss[:, 3 * rows :], width)
    to_core_low[half + LOSS_ROWS :, :] = coded_loss(loss[:, rows : 2 * rows], width)


def rest_kernel(units, text_units, coefs, unit_two, coef_two, to_core, kept, part_two):
    unit = unit_two[...]
    coef = coef_two[...]
    kept[1] = image_part(coefs, text_units, coef, unit, 2)
    kept[0] = image_part(coefs, text_units, coef, unit, 0)
    to_core[...] = image_part(coefs, text_units, coef, unit, 1).astype(BF16)
    part_two[...] = jnp.dot(coef, units[...], preferred_element_type=F32)


def pair_kernel(kept, losses, from_top, from_low, to_across):
    rows = kept.shape[1]
    half = rows // 2
    to_across[:half, :] = (kept[1, :half] + from_top[...].astype(F32)).astype(BF16)
    to_across[half:rows, :] = (kept[1, half:] + from_low[:half, :].astype(F32)).astype(BF16)
    loss = losses[:, 2 * rows : 3 * rows] + decoded_loss(from_low[half : half + LOSS_ROWS, :], rows)
    to_across[rows:, :] = coded_loss(loss, kept.shape[2])


def last_kernel(units, inverses, kept, losses, from_core, from_low, from_across, image_grad, row_loss):
    rows = image_grad.shape[0]
    grad = kept[0] + from_core[...].astype(F32) + from_across[:rows, :].astype(F32)
    wide = units[:rows, :].astype(F32)
    along = jnp.sum(wide * grad, axis=1, keepdims=True)
    image_grad[...] = inverses[:, 0:1] * (grad - wide * along)
    loss = losses[:, :rows] + decoded_loss(from_low[rows // 2 + LOSS_ROWS :, :], rows) + decoded_loss(from_across[rows:, :], rows)
    row_loss[...] = loss / (STEPS * 4 * rows)


def text_kernel(part_two, part_one, part_zero, text_grad):
    text_grad[...] = part_two[...] + part_one[...].astype(F32) + part_zero[...].astype(F32)


def call(kernel, name, outs, arguments, scalars=0, flops=0):
    in_specs = [pl.BlockSpec(memory_space=pltpu.SMEM)] * scalars
    in_specs += [pl.BlockSpec(memory_space=pltpu.VMEM)] * (len(arguments) - scalars)
    moved = sum(a.size * a.dtype.itemsize for a in (*arguments, *outs))
    return pl.pallas_call(
        kernel,
        name=name,
        out_shape=outs,
        in_specs=in_specs,
        out_specs=tuple(pl.BlockSpec(memory_space=pltpu.VMEM) for _ in outs),
        cost_estimate=pl.CostEstimate(flops=flops, bytes_accessed=moved, transcendentals=0),
        compiler_params=pltpu.CompilerParams(vmem_limit_bytes=24 * 1024 * 1024),
    )(*arguments)


def shards(images, texts, log_scale, bias):
    rows, width = images.shape
    span = rows * lax.axis_size("grp")
    tall = rows + LOSS_ROWS
    half = lax.axis_size("blk") // 2
    first_flips = (half - 2, half - 1)
    second_flips = (half - 1, 0)
    made = jax.ShapeDtypeStruct
    texts_one = passed_along(texts, first_flips)
    across = swapped(images, 2)
    core = swapped(images, 1)
    texts_two = passed_along(texts_one, second_flips)
    diagonal = swapped(across, 1)
    matmul = 2 * rows * span * width
    image_unit, text_unit, knobs, inverses = call(
        own_kernel,
        "own_units",
        (made((rows, width), BF16), made((rows, width), BF16), made((2, span), F32), made((rows, 128), F32)),
        (log_scale, bias, images, texts),
        2,
    )
    units, text_units, coefs, losses, part_zero, part_one = call(
        near_kernel,
        "near_texts",
        (
            made((span, width), BF16),
            made((2 * rows, width), BF16),
            made((2 * rows, span), BF16),
            made((1, span), F32),
            made((rows, width), BF16),
            made((rows, width), BF16),
        ),
        (knobs, image_unit, text_unit, core, across, diagonal, texts_one),
        0,
        4 * matmul,
    )
    part_zero = passed_two(part_zero)
    part_one = passed_along(part_one, second_flips)
    coef_two, unit_two, losses, to_core_top, to_core_low = call(
        far_kernel,
        "far_texts",
        (
            made((rows, span), BF16),
            made((rows, width), BF16),
            made((1, span), F32),
            made((rows // 2, width), BF16),
            made((rows // 2 + 2 * LOSS_ROWS, width), BF16),
        ),
        (knobs, units, text_units, coefs, losses, texts_two),
        0,
        2 * matmul,
    )
    from_core_top = swapped(to_core_top, 1)
    from_core_low = swapped(to_core_low, 1)
    to_core_near, kept, part_two = call(
        rest_kernel,
        "image_parts",
        (made((rows, width), BF16), made((2, rows, width), F32), made((rows, width), F32)),
        (units, text_units, coefs, unit_two, coef_two),
    )
    (to_across,) = call(pair_kernel, "chip_sum", (made((tall, width), BF16),), (kept, losses, from_core_top, from_core_low))
    to_across, to_core_near = lax.optimization_barrier((to_across, to_core_near))
    from_across = swapped(to_across, 2)
    from_core_near = swapped(to_core_near, 1)
    (text_grad,) = call(text_kernel, "text_sum", (made((rows, width), F32),), (part_two, part_one, part_zero), 0, 100 * matmul)
    image_grad, row_loss = call(
        last_kernel,
        "image_grad",
        (made((rows, width), F32), made((1, rows), F32)),
        (units, inverses, kept, losses, from_core_near, from_core_low, from_across),
    )
    return (row_loss.reshape(rows), image_grad, text_grad)


def solution(mesh):
    return jax.shard_map(
        shards,
        mesh=mesh,
        in_specs=(P(("blk", "grp"), None), P(("blk", "grp"), None), P(), P()),
        out_specs=(P(("blk", "grp")), P(("blk", "grp"), None), P(("blk", "grp"), None)),
        check_vma=False,
    )
```

```python
import jax
import jax.numpy as jnp
from jax import lax
from jax.experimental import pallas as pl
from jax.experimental.pallas import tpu as pltpu
from jax.sharding import PartitionSpec as P

STEPS = 3
LOSS_ROWS = 16
F32 = jnp.float32
BF16 = jnp.bfloat16


def passed_along(block, flips):
    groups = lax.axis_size("blk")
    members = lax.axis_size("grp")
    route = []
    for group in range(groups):
        flip = 2 if group % (groups // 2) in flips else 0
        for member in range(members):
            target = (group + 1) % groups * members + (member ^ flip)
            route.append((group * members + member, target))
    return lax.ppermute(block, ("blk", "grp"), route)


def passed_two(block):
    groups = lax.axis_size("blk")
    return lax.ppermute(block, "blk", [(i, (i + 2) % groups) for i in range(groups)])


def swapped(block, flip):
    return lax.ppermute(block, "grp", [(i, i ^ flip) for i in range(lax.axis_size("grp"))])


def unit_rows(values):
    wide = values.astype(F32)
    inverse = lax.rsqrt(jnp.sum(wide * wide, axis=-1, keepdims=True) + 1e-06)
    return ((wide * inverse).astype(BF16), inverse)


def pair_terms(text_unit, image_units, scale, bias, positive=None):
    dots = lax.dot_general(
        text_unit, image_units, (((1,), (1,)), ((), ())), preferred_element_type=F32
    )
    logit = scale * dots + bias
    value = logit if positive is None else jnp.where(positive, -logit, logit)
    small = jnp.exp(-jnp.abs(value))
    term = jnp.maximum(value, 0.0) + jnp.log1p(small)
    share = jnp.where(value >= 0.0, 1.0, small) / (1.0 + small)
    coef = share * (scale / STEPS)
    if positive is not None:
        coef = jnp.where(positive, -coef, coef)
    return (jnp.sum(term, axis=0, keepdims=True), coef.astype(BF16))


def by_image(coef, text_unit):
    return lax.dot_general(
        coef, text_unit, (((0,), (0,)), ((), ())), preferred_element_type=F32
    )


def coded_loss(loss, width):
    high = loss.astype(BF16)
    low = (loss - high.astype(F32)).astype(BF16)
    rows = loss.shape[1]
    half = LOSS_ROWS // 2
    parts = [jnp.broadcast_to(part.astype(F32), (half, rows)) for part in (high, low)]
    filled = jnp.concatenate([jnp.concatenate(parts, axis=0), jnp.zeros((LOSS_ROWS, width - rows), F32)], axis=1)
    return filled.astype(BF16)


def decoded_loss(tail, rows):
    wide = tail.astype(F32)
    half = LOSS_ROWS // 2
    return wide[0:1, :rows] + wide[half : half + 1, :rows]


def own_kernel(images, texts, texts_one, image_unit, text_units, inverses, own_images, own_texts, sems):
    copies = [
        pltpu.make_async_copy(images, own_images, sems.at[0]),
        pltpu.make_async_copy(texts, own_texts, sems.at[1]),
    ]
    rows = texts_one.shape[0]
    for copy in copies:
        copy.start()
    text_units[rows:, :] = unit_rows(texts_one[...])[0]
    for copy in copies:
        copy.wait()
    unit, inverse = unit_rows(own_images[...])
    image_unit[...] = unit
    inverses[...] = jnp.broadcast_to(inverse, inverses.shape)
    text_units[:rows, :] = unit_rows(own_texts[...])[0]


def near_kernel(knobs, image_unit, text_units, core, across, diagonal, units, coefs, losses, part_zero, part_one):
    rows = image_unit.shape[0]
    units[:rows, :] = image_unit[...]
    for place, block in ((1, core), (2, across), (3, diagonal)):
        units[place * rows : (place + 1) * rows, :] = unit_rows(block[...])[0]
    scale, offset = knobs[0:1, :], knobs[1:2, :]
    everything = units[...]
    shape = (rows, everything.shape[0])
    positive = lax.broadcasted_iota(jnp.int32, shape, 0) == lax.broadcasted_iota(jnp.int32, shape, 1)
    total = None
    for step, part in enumerate((part_zero, part_one)):
        unit = text_units[step * rows : (step + 1) * rows, :]
        loss, coef = pair_terms(unit, everything, scale, offset, positive if step == 0 else None)
        coefs[step * rows : (step + 1) * rows, :] = coef
        part[...] = jnp.dot(coef, everything, preferred_element_type=F32).astype(BF16)
        total = loss if total is None else total + loss
    losses[...] = total


def image_part(coefs, text_units, coef_two, unit_two, place):
    rows = unit_two.shape[0]
    part = slice(place * rows, (place + 1) * rows)
    return by_image(coefs[:, part], text_units[...]) + by_image(coef_two[:, part], unit_two)


def far_kernel(knobs, units, text_units, coefs, losses, texts_two, coef_out, unit_out, loss_out, to_core_top, to_core_low):
    rows, width = texts_two.shape
    unit_two = unit_rows(texts_two[...])[0]
    loss, coef = pair_terms(unit_two, units[...], knobs[0:1, :], knobs[1:2, :])
    unit_out[...] = unit_two
    coef_out[...] = coef
    loss = losses[...] + loss
    loss_out[...] = loss
    part = image_part(coefs, text_units, coef, unit_two, 3).astype(BF16)
    half = rows // 2
    to_core_top[...] = part[:half]
    to_core_low[:half, :] = part[half:]
    to_core_low[half : half + LOSS_ROWS, :] = coded_loss(loss[:, 3 * rows :], width)
    to_core_low[half + LOSS_ROWS :, :] = coded_loss(loss[:, rows : 2 * rows], width)


def rest_kernel(units, text_units, coefs, unit_two, coef_two, to_core, kept, part_two):
    unit = unit_two[...]
    coef = coef_two[...]
    kept[1] = image_part(coefs, text_units, coef, unit, 2)
    kept[0] = image_part(coefs, text_units, coef, unit, 0)
    to_core[...] = image_part(coefs, text_units, coef, unit, 1).astype(BF16)
    part_two[...] = jnp.dot(coef, units[...], preferred_element_type=F32)


def pair_kernel(kept, losses, from_top, from_low, to_across):
    rows = kept.shape[1]
    half = rows // 2
    to_across[:half, :] = (kept[1, :half] + from_top[...].astype(F32)).astype(BF16)
    to_across[half:rows, :] = (kept[1, half:] + from_low[:half, :].astype(F32)).astype(BF16)
    loss = losses[:, 2 * rows : 3 * rows] + decoded_loss(from_low[half : half + LOSS_ROWS, :], rows)
    to_across[rows:, :] = coded_loss(loss, kept.shape[2])


def last_kernel(units, inverses, kept, losses, from_core, from_low, from_across, image_grad, row_loss):
    rows = image_grad.shape[0]
    grad = kept[0] + from_core[...].astype(F32) + from_across[:rows, :].astype(F32)
    wide = units[:rows, :].astype(F32)
    along = jnp.sum(wide * grad, axis=1, keepdims=True)
    image_grad[...] = inverses[:, 0:1] * (grad - wide * along)
    loss = losses[:, :rows] + decoded_loss(from_low[rows // 2 + LOSS_ROWS :, :], rows) + decoded_loss(from_across[rows:, :], rows)
    row_loss[...] = loss / (STEPS * 4 * rows)


def text_kernel(part_two, part_one, part_zero, text_grad):
    text_grad[...] = part_two[...] + part_one[...].astype(F32) + part_zero[...].astype(F32)


def call(kernel, name, outs, arguments, far=0, flops=0, scratch=()):
    in_specs = [pl.BlockSpec(memory_space=pltpu.HBM)] * far
    in_specs += [pl.BlockSpec(memory_space=pltpu.VMEM)] * (len(arguments) - far)
    moved = sum(a.size * a.dtype.itemsize for a in (*arguments, *outs))
    return pl.pallas_call(
        kernel,
        name=name,
        out_shape=outs,
        in_specs=in_specs,
        out_specs=tuple(pl.BlockSpec(memory_space=pltpu.VMEM) for _ in outs),
        scratch_shapes=scratch,
        cost_estimate=pl.CostEstimate(flops=flops, bytes_accessed=moved, transcendentals=0),
        compiler_params=pltpu.CompilerParams(vmem_limit_bytes=24 * 1024 * 1024),
    )(*arguments)


def shards(images, texts, log_scale, bias):
    rows, width = images.shape
    span = rows * lax.axis_size("grp")
    tall = rows + LOSS_ROWS
    half = lax.axis_size("blk") // 2
    first_flips = (half - 1,)
    second_flips = (0,)
    made = jax.ShapeDtypeStruct
    texts_one = passed_along(texts, first_flips)
    across = swapped(images, 2)
    core = swapped(images, 1)
    texts_two = passed_two(texts)
    pair = jnp.stack([jnp.exp(log_scale), bias])
    knobs = jnp.broadcast_to(pair, (2, span))
    across, knobs = lax.optimization_barrier((across, knobs))
    diagonal = swapped(across, 1)
    matmul = 2 * rows * span * width
    image_unit, text_units, inverses = call(
        own_kernel,
        "own_units",
        (made((rows, width), BF16), made((2 * rows, width), BF16), made((rows, 128), F32)),
        (
            pltpu.with_memory_space_constraint(images, pltpu.HBM),
            pltpu.with_memory_space_constraint(texts, pltpu.HBM),
            texts_one,
        ),
        2,
        30 * matmul,
        (pltpu.VMEM((rows, width), BF16), pltpu.VMEM((rows, width), BF16), pltpu.SemaphoreType.DMA((2,))),
    )
    units, coefs, losses, part_zero, part_one = call(
        near_kernel,
        "near_texts",
        (
            made((span, width), BF16),
            made((2 * rows, span), BF16),
            made((1, span), F32),
            made((rows, width), BF16),
            made((rows, width), BF16),
        ),
        (knobs, image_unit, text_units, core, across, diagonal),
    )
    part_zero = passed_two(part_zero)
    part_one = passed_along(part_one, second_flips)
    coef_two, unit_two, losses, to_core_top, to_core_low = call(
        far_kernel,
        "far_texts",
        (
            made((rows, span), BF16),
            made((rows, width), BF16),
            made((1, span), F32),
            made((rows // 2, width), BF16),
            made((rows // 2 + 2 * LOSS_ROWS, width), BF16),
        ),
        (knobs, units, text_units, coefs, losses, texts_two),
    )
    from_core_top = swapped(to_core_top, 1)
    from_core_low = swapped(to_core_low, 1)
    to_core_near, kept, part_two = call(
        rest_kernel,
        "image_parts",
        (made((rows, width), BF16), made((2, rows, width), F32), made((rows, width), F32)),
        (units, text_units, coefs, unit_two, coef_two),
    )
    (to_across,) = call(pair_kernel, "chip_sum", (made((tall, width), BF16),), (kept, losses, from_core_top, from_core_low))
    to_across, to_core_near = lax.optimization_barrier((to_across, to_core_near))
    from_across = swapped(to_across, 2)
    from_core_near = swapped(to_core_near, 1)
    (text_grad,) = call(text_kernel, "text_sum", (made((rows, width), F32),), (part_two, part_one, part_zero), 0, 20 * matmul)
    image_grad, row_loss = call(
        last_kernel,
        "image_grad",
        (made((rows, width), F32), made((1, rows), F32)),
        (units, inverses, kept, losses, from_core_near, from_core_low, from_across),
    )
    return (row_loss.reshape(rows), image_grad, text_grad)


def solution(mesh):
    return jax.shard_map(
        shards,
        mesh=mesh,
        in_specs=(P(("blk", "grp"), None), P(("blk", "grp"), None), P(), P()),
        out_specs=(P(("blk", "grp")), P(("blk", "grp"), None), P(("blk", "grp"), None)),
        check_vma=False,
    )
```

```python
import jax
import jax.numpy as jnp
from jax import lax
from jax.experimental import pallas as pl
from jax.experimental.pallas import tpu as pltpu
from jax.sharding import PartitionSpec as P

STEPS = 3
LOSS_ROWS = 16
F32 = jnp.float32
BF16 = jnp.bfloat16


def passed_along(block, flips):
    groups = lax.axis_size("blk")
    members = lax.axis_size("grp")
    route = []
    for group in range(groups):
        flip = 2 if group % (groups // 2) in flips else 0
        for member in range(members):
            target = (group + 1) % groups * members + (member ^ flip)
            route.append((group * members + member, target))
    return lax.ppermute(block, ("blk", "grp"), route)


def passed_two(block):
    groups = lax.axis_size("blk")
    return lax.ppermute(block, "blk", [(i, (i + 2) % groups) for i in range(groups)])


def swapped(block, flip):
    return lax.ppermute(block, "grp", [(i, i ^ flip) for i in range(lax.axis_size("grp"))])


def unit_rows(values):
    wide = values.astype(F32)
    inverse = lax.rsqrt(jnp.sum(wide * wide, axis=-1, keepdims=True) + 1e-06)
    return ((wide * inverse).astype(BF16), inverse)


def pair_terms(text_unit, image_units, scale, bias, positive=None):
    dots = lax.dot_general(
        text_unit, image_units, (((1,), (1,)), ((), ())), preferred_element_type=F32
    )
    logit = scale * dots + bias
    value = logit if positive is None else jnp.where(positive, -logit, logit)
    small = jnp.exp(-jnp.abs(value))
    term = jnp.maximum(value, 0.0) + jnp.log1p(small)
    share = jnp.where(value >= 0.0, 1.0, small) / (1.0 + small)
    coef = share * (scale / STEPS)
    if positive is not None:
        coef = jnp.where(positive, -coef, coef)
    return (jnp.sum(term, axis=0, keepdims=True), coef.astype(BF16))


def by_image(coef, text_unit):
    return lax.dot_general(
        coef, text_unit, (((0,), (0,)), ((), ())), preferred_element_type=F32
    )


def coded_loss(loss, width):
    high = loss.astype(BF16)
    low = (loss - high.astype(F32)).astype(BF16)
    rows = loss.shape[1]
    half = LOSS_ROWS // 2
    parts = [jnp.broadcast_to(part.astype(F32), (half, rows)) for part in (high, low)]
    filled = jnp.concatenate([jnp.concatenate(parts, axis=0), jnp.zeros((LOSS_ROWS, width - rows), F32)], axis=1)
    return filled.astype(BF16)


def decoded_loss(tail, rows):
    wide = tail.astype(F32)
    half = LOSS_ROWS // 2
    return wide[0:1, :rows] + wide[half : half + 1, :rows]


def unit_kernel(texts, text_unit):
    text_unit[...] = unit_rows(texts[...])[0]


def own_kernel(images, texts, image_unit, text_unit, inverses, own_images, own_texts, sems):
    copies = [
        pltpu.make_async_copy(images, own_images, sems.at[0]),
        pltpu.make_async_copy(texts, own_texts, sems.at[1]),
    ]
    for copy in copies:
        copy.start()
    for copy in copies:
        copy.wait()
    unit, inverse = unit_rows(own_images[...])
    image_unit[...] = unit
    inverses[...] = jnp.broadcast_to(inverse, inverses.shape)
    text_unit[...] = unit_rows(own_texts[...])[0]


def near_kernel(knobs, image_unit, text_unit, unit_one, core, across, diagonal, units, text_units, coefs, losses, part_zero, part_one):
    rows = image_unit.shape[0]
    units[:rows, :] = image_unit[...]
    for place, block in ((1, core), (2, across), (3, diagonal)):
        units[place * rows : (place + 1) * rows, :] = unit_rows(block[...])[0]
    scale, offset = knobs[0:1, :], knobs[1:2, :]
    everything = units[...]
    shape = (rows, everything.shape[0])
    positive = lax.broadcasted_iota(jnp.int32, shape, 0) == lax.broadcasted_iota(jnp.int32, shape, 1)
    total = None
    for step, (block, part) in enumerate(((text_unit, part_zero), (unit_one, part_one))):
        unit = block[...]
        text_units[step * rows : (step + 1) * rows, :] = unit
        loss, coef = pair_terms(unit, everything, scale, offset, positive if step == 0 else None)
        coefs[step * rows : (step + 1) * rows, :] = coef
        part[...] = jnp.dot(coef, everything, preferred_element_type=F32).astype(BF16)
        total = loss if total is None else total + loss
    losses[...] = total


def image_part(coefs, text_units, coef_two, unit_two, place):
    rows = unit_two.shape[0]
    part = slice(place * rows, (place + 1) * rows)
    return by_image(coefs[:, part], text_units[...]) + by_image(coef_two[:, part], unit_two)


def far_kernel(knobs, units, text_units, coefs, losses, texts_two, coef_out, unit_out, loss_out, to_core_top, to_core_low):
    rows, width = texts_two.shape
    unit_two = unit_rows(texts_two[...])[0]
    loss, coef = pair_terms(unit_two, units[...], knobs[0:1, :], knobs[1:2, :])
    unit_out[...] = unit_two
    coef_out[...] = coef
    loss = losses[...] + loss
    loss_out[...] = loss
    part = image_part(coefs, text_units, coef, unit_two, 3).astype(BF16)
    half = rows // 2
    to_core_top[...] = part[:half]
    to_core_low[:half, :] = part[half:]
    to_core_low[half : half + LOSS_ROWS, :] = coded_loss(loss[:, 3 * rows :], width)
    to_core_low[half + LOSS_ROWS :, :] = coded_loss(loss[:, rows : 2 * rows], width)


def rest_kernel(units, text_units, coefs, unit_two, coef_two, to_core, kept, part_two):
    unit = unit_two[...]
    coef = coef_two[...]
    kept[1] = image_part(coefs, text_units, coef, unit, 2)
    kept[0] = image_part(coefs, text_units, coef, unit, 0)
    to_core[...] = image_part(coefs, text_units, coef, unit, 1).astype(BF16)
    part_two[...] = jnp.dot(coef, units[...], preferred_element_type=F32)


def pair_kernel(kept, losses, from_top, from_low, to_across, loss_across):
    rows = kept.shape[1]
    half = rows // 2
    to_across[:half, :] = (kept[1, :half] + from_top[...].astype(F32)).astype(BF16)
    to_across[half:, :] = (kept[1, half:] + from_low[:half, :].astype(F32)).astype(BF16)
    loss_across[...] = losses[:, 2 * rows : 3 * rows] + decoded_loss(from_low[half : half + LOSS_ROWS, :], rows)


def last_kernel(from_across, from_core, loss_across, from_low, units, inverses, kept, losses, image_grad, row_loss):
    rows = image_grad.shape[0]
    grad = kept[0] + from_core[...].astype(F32) + from_across[...].astype(F32)
    wide = units[:rows, :].astype(F32)
    along = jnp.sum(wide * grad, axis=1, keepdims=True)
    image_grad[...] = inverses[:, 0:1] * (grad - wide * along)
    loss = losses[:, :rows] + loss_across[...] + decoded_loss(from_low[rows // 2 + LOSS_ROWS :, :], rows)
    row_loss[...] = loss / (STEPS * 4 * rows)


def text_kernel(part_zero, part_one, part_two, text_grad):
    text_grad[...] = part_two[...] + part_one[...].astype(F32) + part_zero[...].astype(F32)


def call(kernel, name, outs, arguments, far=0, flops=0, scratch=()):
    in_specs = [pl.BlockSpec(memory_space=pltpu.HBM)] * far
    in_specs += [pl.BlockSpec(memory_space=pltpu.VMEM)] * (len(arguments) - far)
    moved = sum(a.size * a.dtype.itemsize for a in (*arguments, *outs))
    return pl.pallas_call(
        kernel,
        name=name,
        out_shape=outs,
        in_specs=in_specs,
        out_specs=tuple(pl.BlockSpec(memory_space=pltpu.VMEM) for _ in outs),
        scratch_shapes=scratch,
        cost_estimate=pl.CostEstimate(flops=flops, bytes_accessed=moved, transcendentals=0),
        compiler_params=pltpu.CompilerParams(vmem_limit_bytes=24 * 1024 * 1024),
    )(*arguments)


def shards(images, texts, log_scale, bias):
    rows, width = images.shape
    span = rows * lax.axis_size("grp")
    half = lax.axis_size("blk") // 2
    first_flips = (half - 2, half - 1)
    second_flips = (half - 1, 0)
    made = jax.ShapeDtypeStruct
    texts_one = passed_along(texts, first_flips)
    across = swapped(images, 2)
    core = swapped(images, 1)
    texts_two = passed_two(texts)
    pair = jnp.stack([jnp.exp(log_scale), bias])
    knobs = jnp.broadcast_to(pair, (2, span))
    across, knobs = lax.optimization_barrier((across, knobs))
    diagonal = swapped(across, 1)
    matmul = 2 * rows * span * width
    (unit_one,) = call(unit_kernel, "next_units", (made((rows, width), BF16),), (texts_one,), 0, 30 * matmul)
    image_unit, text_unit, inverses = call(
        own_kernel,
        "own_units",
        (made((rows, width), BF16), made((rows, width), BF16), made((rows, 128), F32)),
        (
            pltpu.with_memory_space_constraint(images, pltpu.HBM),
            pltpu.with_memory_space_constraint(texts, pltpu.HBM),
        ),
        2,
        0 * matmul,
        (pltpu.VMEM((rows, width), BF16), pltpu.VMEM((rows, width), BF16), pltpu.SemaphoreType.DMA((2,))),
    )
    units, text_units, coefs, losses, part_zero, part_one = call(
        near_kernel,
        "near_texts",
        (
            made((span, width), BF16),
            made((2 * rows, width), BF16),
            made((2 * rows, span), BF16),
            made((1, span), F32),
            made((rows, width), BF16),
            made((rows, width), BF16),
        ),
        (knobs, image_unit, text_unit, unit_one, core, across, diagonal),
    )
    part_zero = passed_two(part_zero)
    part_one = passed_along(part_one, second_flips)
    coef_two, unit_two, losses, to_core_top, to_core_low = call(
        far_kernel,
        "far_texts",
        (
            made((rows, span), BF16),
            made((rows, width), BF16),
            made((1, span), F32),
            made((rows // 2, width), BF16),
            made((rows // 2 + 2 * LOSS_ROWS, width), BF16),
        ),
        (knobs, units, text_units, coefs, losses, texts_two),
    )
    from_core_top = swapped(to_core_top, 1)
    from_core_low = swapped(to_core_low, 1)
    to_core_near, kept, part_two = call(
        rest_kernel,
        "image_parts",
        (made((rows, width), BF16), made((2, rows, width), F32), made((rows, width), F32)),
        (units, text_units, coefs, unit_two, coef_two),
    )
    to_across, loss_across = call(
        pair_kernel,
        "chip_sum",
        (made((rows, width), BF16), made((1, rows), F32)),
        (kept, losses, from_core_top, from_core_low),
    )
    to_across, to_core_near = lax.optimization_barrier((to_across, to_core_near))
    from_across = swapped(to_across, 2)
    from_core_near = swapped(to_core_near, 1)
    loss_across = swapped(loss_across, 2)
    (text_grad,) = call(text_kernel, "text_sum", (made((rows, width), F32),), (part_zero, part_one, part_two), 0, 20 * matmul)
    image_grad, row_loss = call(
        last_kernel,
        "image_grad",
        (made((rows, width), F32), made((1, rows), F32)),
        (from_across, from_core_near, loss_across, from_core_low, units, inverses, kept, losses),
    )
    return (row_loss.reshape(rows), image_grad, text_grad)


def solution(mesh):
    return jax.shard_map(
        shards,
        mesh=mesh,
        in_specs=(P(("blk", "grp"), None), P(("blk", "grp"), None), P(), P()),
        out_specs=(P(("blk", "grp")), P(("blk", "grp"), None), P(("blk", "grp"), None)),
        check_vma=False,
    )
```

```python
import jax
import jax.numpy as jnp
from jax import lax
from jax.experimental import pallas as pl
from jax.experimental.pallas import tpu as pltpu
from jax.sharding import PartitionSpec as P

STEPS = 3
LOSS_ROWS = 16
F32 = jnp.float32
BF16 = jnp.bfloat16


def passed_along(block, flips):
    groups = lax.axis_size("blk")
    members = lax.axis_size("grp")
    route = []
    for group in range(groups):
        flip = 2 if group % (groups // 2) in flips else 0
        for member in range(members):
            target = (group + 1) % groups * members + (member ^ flip)
            route.append((group * members + member, target))
    return lax.ppermute(block, ("blk", "grp"), route)


def passed_two(block):
    groups = lax.axis_size("blk")
    return lax.ppermute(block, "blk", [(i, (i + 2) % groups) for i in range(groups)])


def swapped(block, flip):
    return lax.ppermute(block, "grp", [(i, i ^ flip) for i in range(lax.axis_size("grp"))])


def unit_rows(values):
    wide = values.astype(F32)
    inverse = lax.rsqrt(jnp.sum(wide * wide, axis=-1, keepdims=True) + 1e-06)
    return ((wide * inverse).astype(BF16), inverse)


def pair_terms(text_unit, image_units, scale, bias, positive=None):
    dots = lax.dot_general(
        text_unit, image_units, (((1,), (1,)), ((), ())), preferred_element_type=F32
    )
    logit = scale * dots + bias
    value = logit if positive is None else jnp.where(positive, -logit, logit)
    small = jnp.exp(-jnp.abs(value))
    term = jnp.maximum(value, 0.0) + jnp.log1p(small)
    share = jnp.where(value >= 0.0, 1.0, small) / (1.0 + small)
    coef = share * (scale / STEPS)
    if positive is not None:
        coef = jnp.where(positive, -coef, coef)
    return (jnp.sum(term, axis=0, keepdims=True), coef.astype(BF16))


def by_image(coef, text_unit):
    return lax.dot_general(
        coef, text_unit, (((0,), (0,)), ((), ())), preferred_element_type=F32
    )


def coded_loss(loss, width):
    high = loss.astype(BF16)
    low = (loss - high.astype(F32)).astype(BF16)
    rows = loss.shape[1]
    half = LOSS_ROWS // 2
    parts = [jnp.broadcast_to(part.astype(F32), (half, rows)) for part in (high, low)]
    filled = jnp.concatenate([jnp.concatenate(parts, axis=0), jnp.zeros((LOSS_ROWS, width - rows), F32)], axis=1)
    return filled.astype(BF16)


def decoded_loss(tail, rows):
    wide = tail.astype(F32)
    half = LOSS_ROWS // 2
    return wide[0:1, :rows] + wide[half : half + 1, :rows]


def unit_kernel(texts, text_unit):
    text_unit[...] = unit_rows(texts[...])[0]


def own_kernel(images, texts, image_unit, text_unit, inverses, own_images, own_texts, sems):
    copies = [
        pltpu.make_async_copy(images, own_images, sems.at[0]),
        pltpu.make_async_copy(texts, own_texts, sems.at[1]),
    ]
    for copy in copies:
        copy.start()
    for copy in copies:
        copy.wait()
    unit, inverse = unit_rows(own_images[...])
    image_unit[...] = unit
    inverses[...] = jnp.broadcast_to(inverse, inverses.shape)
    text_unit[...] = unit_rows(own_texts[...])[0]


def near_kernel(knobs, image_unit, text_unit, unit_one, core, across, diagonal, units, text_units, coefs, losses, part_zero, part_one):
    rows = image_unit.shape[0]
    units[:rows, :] = image_unit[...]
    for place, block in ((1, core), (2, across), (3, diagonal)):
        units[place * rows : (place + 1) * rows, :] = unit_rows(block[...])[0]
    scale, offset = knobs[0:1, :], knobs[1:2, :]
    everything = units[...]
    shape = (rows, everything.shape[0])
    positive = lax.broadcasted_iota(jnp.int32, shape, 0) == lax.broadcasted_iota(jnp.int32, shape, 1)
    total = None
    for step, (block, part) in enumerate(((text_unit, part_zero), (unit_one, part_one))):
        unit = block[...]
        text_units[step * rows : (step + 1) * rows, :] = unit
        loss, coef = pair_terms(unit, everything, scale, offset, positive if step == 0 else None)
        coefs[step * rows : (step + 1) * rows, :] = coef
        part[...] = jnp.dot(coef, everything, preferred_element_type=F32).astype(BF16)
        total = loss if total is None else total + loss
    losses[...] = total


def image_part(coefs, text_units, coef_two, unit_two, place):
    rows = unit_two.shape[0]
    part = slice(place * rows, (place + 1) * rows)
    return by_image(coefs[:, part], text_units[...]) + by_image(coef_two[:, part], unit_two)


def far_kernel(knobs, units, text_units, coefs, losses, texts_two, coef_out, unit_out, loss_out, to_core_top, to_core_low):
    rows, width = texts_two.shape
    unit_two = unit_rows(texts_two[...])[0]
    loss, coef = pair_terms(unit_two, units[...], knobs[0:1, :], knobs[1:2, :])
    unit_out[...] = unit_two
    coef_out[...] = coef
    loss = losses[...] + loss
    loss_out[...] = loss
    part = image_part(coefs, text_units, coef, unit_two, 3).astype(BF16)
    half = rows // 2
    to_core_top[...] = part[:half]
    to_core_low[:half, :] = part[half:]
    to_core_low[half : half + LOSS_ROWS, :] = coded_loss(loss[:, 3 * rows :], width)
    to_core_low[half + LOSS_ROWS :, :] = coded_loss(loss[:, rows : 2 * rows], width)


def rest_kernel(units, text_units, coefs, unit_two, coef_two, to_core, kept, part_two):
    unit = unit_two[...]
    coef = coef_two[...]
    kept[1] = image_part(coefs, text_units, coef, unit, 2)
    kept[0] = image_part(coefs, text_units, coef, unit, 0)
    to_core[...] = image_part(coefs, text_units, coef, unit, 1).astype(BF16)
    part_two[...] = jnp.dot(coef, units[...], preferred_element_type=F32)


def pair_kernel(kept, losses, from_top, from_low, to_across, loss_across):
    rows = kept.shape[1]
    half = rows // 2
    to_across[:half, :] = (kept[1, :half] + from_top[...].astype(F32)).astype(BF16)
    to_across[half:, :] = (kept[1, half:] + from_low[:half, :].astype(F32)).astype(BF16)
    loss_across[...] = losses[:, 2 * rows : 3 * rows] + decoded_loss(from_low[half : half + LOSS_ROWS, :], rows)


def last_kernel(from_across, from_core, loss_across, from_low, units, inverses, kept, losses, image_grad, row_loss):
    rows = image_grad.shape[0]
    grad = kept[0] + from_core[...].astype(F32) + from_across[...].astype(F32)
    wide = units[:rows, :].astype(F32)
    along = jnp.sum(wide * grad, axis=1, keepdims=True)
    image_grad[...] = inverses[:, 0:1] * (grad - wide * along)
    loss = losses[:, :rows] + loss_across[...] + decoded_loss(from_low[rows // 2 + LOSS_ROWS :, :], rows)
    row_loss[...] = loss / (STEPS * 4 * rows)


def text_kernel(part_zero, part_one, part_two, text_grad):
    text_grad[...] = part_two[...] + part_one[...].astype(F32) + part_zero[...].astype(F32)


def call(kernel, name, outs, arguments, far=0, flops=0, scratch=()):
    in_specs = [pl.BlockSpec(memory_space=pltpu.HBM)] * far
    in_specs += [pl.BlockSpec(memory_space=pltpu.VMEM)] * (len(arguments) - far)
    moved = sum(a.size * a.dtype.itemsize for a in (*arguments, *outs))
    return pl.pallas_call(
        kernel,
        name=name,
        out_shape=outs,
        in_specs=in_specs,
        out_specs=tuple(pl.BlockSpec(memory_space=pltpu.VMEM) for _ in outs),
        scratch_shapes=scratch,
        cost_estimate=pl.CostEstimate(flops=flops, bytes_accessed=moved, transcendentals=0),
        compiler_params=pltpu.CompilerParams(vmem_limit_bytes=24 * 1024 * 1024),
    )(*arguments)


def shards(images, texts, log_scale, bias):
    rows, width = images.shape
    span = rows * lax.axis_size("grp")
    half = lax.axis_size("blk") // 2
    first_flips = (half - 2,)
    second_flips = (half - 1,)
    made = jax.ShapeDtypeStruct
    texts_one = passed_along(texts, first_flips)
    across = swapped(images, 2)
    core = swapped(images, 1)
    texts_two = passed_two(texts)
    pair = jnp.stack([jnp.exp(log_scale), bias])
    knobs = jnp.broadcast_to(pair, (2, span))
    across, knobs = lax.optimization_barrier((across, knobs))
    diagonal = swapped(across, 1)
    matmul = 2 * rows * span * width
    (unit_one,) = call(unit_kernel, "next_units", (made((rows, width), BF16),), (texts_one,), 0, 30 * matmul)
    image_unit, text_unit, inverses = call(
        own_kernel,
        "own_units",
        (made((rows, width), BF16), made((rows, width), BF16), made((rows, 128), F32)),
        (
            pltpu.with_memory_space_constraint(images, pltpu.HBM),
            pltpu.with_memory_space_constraint(texts, pltpu.HBM),
        ),
        2,
        0 * matmul,
        (pltpu.VMEM((rows, width), BF16), pltpu.VMEM((rows, width), BF16), pltpu.SemaphoreType.DMA((2,))),
    )
    units, text_units, coefs, losses, part_zero, part_one = call(
        near_kernel,
        "near_texts",
        (
            made((span, width), BF16),
            made((2 * rows, width), BF16),
            made((2 * rows, span), BF16),
            made((1, span), F32),
            made((rows, width), BF16),
            made((rows, width), BF16),
        ),
        (knobs, image_unit, text_unit, unit_one, core, across, diagonal),
    )
    part_zero = passed_two(part_zero)
    part_one = passed_along(part_one, second_flips)
    coef_two, unit_two, losses, to_core_top, to_core_low = call(
        far_kernel,
        "far_texts",
        (
            made((rows, span), BF16),
            made((rows, width), BF16),
            made((1, span), F32),
            made((rows // 2, width), BF16),
            made((rows // 2 + 2 * LOSS_ROWS, width), BF16),
        ),
        (knobs, units, text_units, coefs, losses, texts_two),
    )
    from_core_top = swapped(to_core_top, 1)
    from_core_low = swapped(to_core_low, 1)
    to_core_near, kept, part_two = call(
        rest_kernel,
        "image_parts",
        (made((rows, width), BF16), made((2, rows, width), F32), made((rows, width), F32)),
        (units, text_units, coefs, unit_two, coef_two),
    )
    to_across, loss_across = call(
        pair_kernel,
        "chip_sum",
        (made((rows, width), BF16), made((1, rows), F32)),
        (kept, losses, from_core_top, from_core_low),
    )
    to_across, to_core_near = lax.optimization_barrier((to_across, to_core_near))
    from_across = swapped(to_across, 2)
    from_core_near = swapped(to_core_near, 1)
    loss_across = swapped(loss_across, 2)
    (text_grad,) = call(text_kernel, "text_sum", (made((rows, width), F32),), (part_zero, part_one, part_two), 0, 20 * matmul)
    image_grad, row_loss = call(
        last_kernel,
        "image_grad",
        (made((rows, width), F32), made((1, rows), F32)),
        (from_across, from_core_near, loss_across, from_core_low, units, inverses, kept, losses),
    )
    return (row_loss.reshape(rows), image_grad, text_grad)


def solution(mesh):
    return jax.shard_map(
        shards,
        mesh=mesh,
        in_specs=(P(("blk", "grp"), None), P(("blk", "grp"), None), P(), P()),
        out_specs=(P(("blk", "grp")), P(("blk", "grp"), None), P(("blk", "grp"), None)),
        check_vma=False,
    )
```

```python
import jax
import jax.numpy as jnp
from jax import lax
from jax.experimental import pallas as pl
from jax.experimental.pallas import tpu as pltpu
from jax.sharding import PartitionSpec as P

STEPS = 3
LOSS_ROWS = 16
F32 = jnp.float32
BF16 = jnp.bfloat16


def passed_along(block, flips):
    groups = lax.axis_size("blk")
    members = lax.axis_size("grp")
    route = []
    for group in range(groups):
        flip = 2 if group % (groups // 2) in flips else 0
        for member in range(members):
            target = (group + 1) % groups * members + (member ^ flip)
            route.append((group * members + member, target))
    return lax.ppermute(block, ("blk", "grp"), route)


def passed_two(block):
    groups = lax.axis_size("blk")
    return lax.ppermute(block, "blk", [(i, (i + 2) % groups) for i in range(groups)])


def swapped(block, flip):
    return lax.ppermute(block, "grp", [(i, i ^ flip) for i in range(lax.axis_size("grp"))])


def unit_rows(values):
    wide = values.astype(F32)
    inverse = lax.rsqrt(jnp.sum(wide * wide, axis=-1, keepdims=True) + 1e-06)
    return ((wide * inverse).astype(BF16), inverse)


def pair_terms(text_unit, image_units, scale, bias, positive=None):
    dots = lax.dot_general(
        text_unit, image_units, (((1,), (1,)), ((), ())), preferred_element_type=F32
    )
    logit = scale * dots + bias
    value = logit if positive is None else jnp.where(positive, -logit, logit)
    small = jnp.exp(-jnp.abs(value))
    term = jnp.maximum(value, 0.0) + jnp.log1p(small)
    share = jnp.where(value >= 0.0, 1.0, small) / (1.0 + small)
    coef = share * (scale / STEPS)
    if positive is not None:
        coef = jnp.where(positive, -coef, coef)
    return (jnp.sum(term, axis=0, keepdims=True), coef.astype(BF16))


def by_image(coef, text_unit):
    return lax.dot_general(
        coef, text_unit, (((0,), (0,)), ((), ())), preferred_element_type=F32
    )


def coded_loss(loss, width):
    high = loss.astype(BF16)
    low = (loss - high.astype(F32)).astype(BF16)
    rows = loss.shape[1]
    half = LOSS_ROWS // 2
    parts = [jnp.broadcast_to(part.astype(F32), (half, rows)) for part in (high, low)]
    filled = jnp.concatenate([jnp.concatenate(parts, axis=0), jnp.zeros((LOSS_ROWS, width - rows), F32)], axis=1)
    return filled.astype(BF16)


def decoded_loss(tail, rows):
    wide = tail.astype(F32)
    half = LOSS_ROWS // 2
    return wide[0:1, :rows] + wide[half : half + 1, :rows]


def unit_kernel(texts, text_unit):
    text_unit[...] = unit_rows(texts[...])[0]


def own_kernel(images, texts, image_unit, text_unit, inverses, own_images, own_texts, sems):
    copies = [
        pltpu.make_async_copy(images, own_images, sems.at[0]),
        pltpu.make_async_copy(texts, own_texts, sems.at[1]),
    ]
    for copy in copies:
        copy.start()
    for copy in copies:
        copy.wait()
    unit, inverse = unit_rows(own_images[...])
    image_unit[...] = unit
    inverses[...] = jnp.broadcast_to(inverse, inverses.shape)
    text_unit[...] = unit_rows(own_texts[...])[0]


def same_kernel(knobs, image_unit, text_unit, unit_one, core, across, diagonal, units, text_units, coef_out, losses, part_zero):
    rows = image_unit.shape[0]
    units[:rows, :] = image_unit[...]
    for place, block in ((1, core), (2, across), (3, diagonal)):
        units[place * rows : (place + 1) * rows, :] = unit_rows(block[...])[0]
    unit = text_unit[...]
    text_units[:rows, :] = unit
    text_units[rows:, :] = unit_one[...]
    everything = units[...]
    shape = (rows, everything.shape[0])
    positive = lax.broadcasted_iota(jnp.int32, shape, 0) == lax.broadcasted_iota(jnp.int32, shape, 1)
    loss, coef = pair_terms(unit, everything, knobs[0:1, :], knobs[1:2, :], positive)
    coef_out[...] = coef
    losses[...] = loss
    part_zero[...] = jnp.dot(coef, everything, preferred_element_type=F32).astype(BF16)


def next_kernel(knobs, units, text_units, coef_zero, loss_zero, coefs, losses, part_one):
    rows = coef_zero.shape[0]
    everything = units[...]
    loss, coef = pair_terms(text_units[rows:, :], everything, knobs[0:1, :], knobs[1:2, :])
    coefs[:rows, :] = coef_zero[...]
    coefs[rows:, :] = coef
    losses[...] = loss_zero[...] + loss
    part_one[...] = jnp.dot(coef, everything, preferred_element_type=F32).astype(BF16)


def image_part(coefs, text_units, coef_two, unit_two, place):
    rows = unit_two.shape[0]
    part = slice(place * rows, (place + 1) * rows)
    return by_image(coefs[:, part], text_units[...]) + by_image(coef_two[:, part], unit_two)


def far_kernel(knobs, units, text_units, coefs, losses, texts_two, coef_out, unit_out, loss_out, to_core_top, to_core_low):
    rows, width = texts_two.shape
    unit_two = unit_rows(texts_two[...])[0]
    loss, coef = pair_terms(unit_two, units[...], knobs[0:1, :], knobs[1:2, :])
    unit_out[...] = unit_two
    coef_out[...] = coef
    loss = losses[...] + loss
    loss_out[...] = loss
    part = image_part(coefs, text_units, coef, unit_two, 3).astype(BF16)
    half = rows // 2
    to_core_top[...] = part[:half]
    to_core_low[:half, :] = part[half:]
    to_core_low[half : half + LOSS_ROWS, :] = coded_loss(loss[:, 3 * rows :], width)
    to_core_low[half + LOSS_ROWS :, :] = coded_loss(loss[:, rows : 2 * rows], width)


def rest_kernel(units, text_units, coefs, unit_two, coef_two, to_core, kept, part_two):
    unit = unit_two[...]
    coef = coef_two[...]
    kept[1] = image_part(coefs, text_units, coef, unit, 2)
    kept[0] = image_part(coefs, text_units, coef, unit, 0)
    to_core[...] = image_part(coefs, text_units, coef, unit, 1).astype(BF16)
    part_two[...] = jnp.dot(coef, units[...], preferred_element_type=F32)


def pair_kernel(kept, losses, from_top, from_low, to_across, loss_across):
    rows = kept.shape[1]
    half = rows // 2
    to_across[:half, :] = (kept[1, :half] + from_top[...].astype(F32)).astype(BF16)
    to_across[half:, :] = (kept[1, half:] + from_low[:half, :].astype(F32)).astype(BF16)
    loss_across[...] = losses[:, 2 * rows : 3 * rows] + decoded_loss(from_low[half : half + LOSS_ROWS, :], rows)


def last_kernel(from_across, from_core, loss_across, from_low, units, inverses, kept, losses, image_grad, row_loss):
    rows = image_grad.shape[0]
    grad = kept[0] + from_core[...].astype(F32) + from_across[...].astype(F32)
    wide = units[:rows, :].astype(F32)
    along = jnp.sum(wide * grad, axis=1, keepdims=True)
    image_grad[...] = inverses[:, 0:1] * (grad - wide * along)
    loss = losses[:, :rows] + loss_across[...] + decoded_loss(from_low[rows // 2 + LOSS_ROWS :, :], rows)
    row_loss[...] = loss / (STEPS * 4 * rows)


def text_kernel(part_zero, part_one, part_two, text_grad):
    text_grad[...] = part_two[...] + part_one[...].astype(F32) + part_zero[...].astype(F32)


def call(kernel, name, outs, arguments, far=0, flops=0, scratch=()):
    in_specs = [pl.BlockSpec(memory_space=pltpu.HBM)] * far
    in_specs += [pl.BlockSpec(memory_space=pltpu.VMEM)] * (len(arguments) - far)
    moved = sum(a.size * a.dtype.itemsize for a in (*arguments, *outs))
    return pl.pallas_call(
        kernel,
        name=name,
        out_shape=outs,
        in_specs=in_specs,
        out_specs=tuple(pl.BlockSpec(memory_space=pltpu.VMEM) for _ in outs),
        scratch_shapes=scratch,
        cost_estimate=pl.CostEstimate(flops=flops, bytes_accessed=moved, transcendentals=0),
        compiler_params=pltpu.CompilerParams(vmem_limit_bytes=24 * 1024 * 1024),
    )(*arguments)


def shards(images, texts, log_scale, bias):
    rows, width = images.shape
    span = rows * lax.axis_size("grp")
    half = lax.axis_size("blk") // 2
    first_flips = (half - 2,)
    second_flips = (half - 1,)
    made = jax.ShapeDtypeStruct
    texts_one = passed_along(texts, first_flips)
    across = swapped(images, 2)
    core = swapped(images, 1)
    texts_two = passed_two(texts)
    pair = jnp.stack([jnp.exp(log_scale), bias])
    knobs = jnp.broadcast_to(pair, (2, span))
    across, knobs = lax.optimization_barrier((across, knobs))
    diagonal = swapped(across, 1)
    matmul = 2 * rows * span * width
    (unit_one,) = call(unit_kernel, "next_units", (made((rows, width), BF16),), (texts_one,), 0, 30 * matmul)
    image_unit, text_unit, inverses = call(
        own_kernel,
        "own_units",
        (made((rows, width), BF16), made((rows, width), BF16), made((rows, 128), F32)),
        (
            pltpu.with_memory_space_constraint(images, pltpu.HBM),
            pltpu.with_memory_space_constraint(texts, pltpu.HBM),
        ),
        2,
        0 * matmul,
        (pltpu.VMEM((rows, width), BF16), pltpu.VMEM((rows, width), BF16), pltpu.SemaphoreType.DMA((2,))),
    )
    units, text_units, coef_zero, loss_zero, part_zero = call(
        same_kernel,
        "same_texts",
        (
            made((span, width), BF16),
            made((2 * rows, width), BF16),
            made((rows, span), BF16),
            made((1, span), F32),
            made((rows, width), BF16),
        ),
        (knobs, image_unit, text_unit, unit_one, core, across, diagonal),
    )
    part_zero = passed_two(part_zero)
    coefs, losses, part_one = call(
        next_kernel,
        "next_texts",
        (made((2 * rows, span), BF16), made((1, span), F32), made((rows, width), BF16)),
        (knobs, units, text_units, coef_zero, loss_zero),
    )
    part_one = passed_along(part_one, second_flips)
    coef_two, unit_two, losses, to_core_top, to_core_low = call(
        far_kernel,
        "far_texts",
        (
            made((rows, span), BF16),
            made((rows, width), BF16),
            made((1, span), F32),
            made((rows // 2, width), BF16),
            made((rows // 2 + 2 * LOSS_ROWS, width), BF16),
        ),
        (knobs, units, text_units, coefs, losses, texts_two),
    )
    from_core_top = swapped(to_core_top, 1)
    from_core_low = swapped(to_core_low, 1)
    to_core_near, kept, part_two = call(
        rest_kernel,
        "image_parts",
        (made((rows, width), BF16), made((2, rows, width), F32), made((rows, width), F32)),
        (units, text_units, coefs, unit_two, coef_two),
    )
    to_across, loss_across = call(
        pair_kernel,
        "chip_sum",
        (made((rows, width), BF16), made((1, rows), F32)),
        (kept, losses, from_core_top, from_core_low),
    )
    to_across, to_core_near = lax.optimization_barrier((to_across, to_core_near))
    from_across = swapped(to_across, 2)
    from_core_near = swapped(to_core_near, 1)
    loss_across = swapped(loss_across, 2)
    (text_grad,) = call(text_kernel, "text_sum", (made((rows, width), F32),), (part_zero, part_one, part_two), 0, 20 * matmul)
    image_grad, row_loss = call(
        last_kernel,
        "image_grad",
        (made((rows, width), F32), made((1, rows), F32)),
        (from_across, from_core_near, loss_across, from_core_low, units, inverses, kept, losses),
    )
    return (row_loss.reshape(rows), image_grad, text_grad)


def solution(mesh):
    return jax.shard_map(
        shards,
        mesh=mesh,
        in_specs=(P(("blk", "grp"), None), P(("blk", "grp"), None), P(), P()),
        out_specs=(P(("blk", "grp")), P(("blk", "grp"), None), P(("blk", "grp"), None)),
        check_vma=False,
    )
```

```python
import jax
import jax.numpy as jnp
from jax import lax
from jax.experimental import pallas as pl
from jax.experimental.pallas import tpu as pltpu
from jax.sharding import PartitionSpec as P

STEPS = 3
LOSS_ROWS = 16
F32 = jnp.float32
BF16 = jnp.bfloat16


def passed_along(block, flips):
    groups = lax.axis_size("blk")
    members = lax.axis_size("grp")
    route = []
    for group in range(groups):
        flip = 2 if group % (groups // 2) in flips else 0
        for member in range(members):
            target = (group + 1) % groups * members + (member ^ flip)
            route.append((group * members + member, target))
    return lax.ppermute(block, ("blk", "grp"), route)


def passed_two(block):
    groups = lax.axis_size("blk")
    return lax.ppermute(block, "blk", [(i, (i + 2) % groups) for i in range(groups)])


def swapped(block, flip):
    return lax.ppermute(block, "grp", [(i, i ^ flip) for i in range(lax.axis_size("grp"))])


def unit_rows(values):
    wide = values.astype(F32)
    inverse = lax.rsqrt(jnp.sum(wide * wide, axis=-1, keepdims=True) + 1e-06)
    return ((wide * inverse).astype(BF16), inverse)


def pair_terms(text_unit, image_units, scale, bias, positive=None):
    dots = lax.dot_general(
        text_unit, image_units, (((1,), (1,)), ((), ())), preferred_element_type=F32
    )
    logit = scale * dots + bias
    value = logit if positive is None else jnp.where(positive, -logit, logit)
    small = jnp.exp(-jnp.abs(value))
    term = jnp.maximum(value, 0.0) + jnp.log1p(small)
    share = jnp.where(value >= 0.0, 1.0, small) / (1.0 + small)
    coef = share * (scale / STEPS)
    if positive is not None:
        coef = jnp.where(positive, -coef, coef)
    return (jnp.sum(term, axis=0, keepdims=True), coef.astype(BF16))


def by_image(coef, text_unit):
    return lax.dot_general(
        coef, text_unit, (((0,), (0,)), ((), ())), preferred_element_type=F32
    )


def coded_loss(loss, width):
    high = loss.astype(BF16)
    low = (loss - high.astype(F32)).astype(BF16)
    rows = loss.shape[1]
    half = LOSS_ROWS // 2
    parts = [jnp.broadcast_to(part.astype(F32), (half, rows)) for part in (high, low)]
    filled = jnp.concatenate([jnp.concatenate(parts, axis=0), jnp.zeros((LOSS_ROWS, width - rows), F32)], axis=1)
    return filled.astype(BF16)


def decoded_loss(tail, rows):
    wide = tail.astype(F32)
    half = LOSS_ROWS // 2
    return wide[0:1, :rows] + wide[half : half + 1, :rows]


def unit_kernel(texts, text_unit):
    text_unit[...] = unit_rows(texts[...])[0]


def own_kernel(images, texts, image_unit, text_unit, inverses, own_images, own_texts, sems):
    copies = [
        pltpu.make_async_copy(images, own_images, sems.at[0]),
        pltpu.make_async_copy(texts, own_texts, sems.at[1]),
    ]
    for copy in copies:
        copy.start()
    for copy in copies:
        copy.wait()
    unit, inverse = unit_rows(own_images[...])
    image_unit[...] = unit
    inverses[...] = jnp.broadcast_to(inverse, inverses.shape)
    text_unit[...] = unit_rows(own_texts[...])[0]


def same_kernel(knobs, image_unit, text_unit, unit_one, core, across, diagonal, units, text_units, coef_out, losses, part_zero):
    rows = image_unit.shape[0]
    units[:rows, :] = image_unit[...]
    for place, block in ((1, core), (2, across), (3, diagonal)):
        units[place * rows : (place + 1) * rows, :] = unit_rows(block[...])[0]
    unit = text_unit[...]
    text_units[:rows, :] = unit
    text_units[rows:, :] = unit_one[...]
    everything = units[...]
    shape = (rows, everything.shape[0])
    positive = lax.broadcasted_iota(jnp.int32, shape, 0) == lax.broadcasted_iota(jnp.int32, shape, 1)
    loss, coef = pair_terms(unit, everything, knobs[0:1, :], knobs[1:2, :], positive)
    coef_out[...] = coef
    losses[...] = loss
    part_zero[...] = jnp.dot(coef, everything, preferred_element_type=F32).astype(BF16)


def next_kernel(knobs, units, text_units, coef_zero, loss_zero, coefs, losses, part_one):
    rows = coef_zero.shape[0]
    everything = units[...]
    loss, coef = pair_terms(text_units[rows:, :], everything, knobs[0:1, :], knobs[1:2, :])
    coefs[:rows, :] = coef_zero[...]
    coefs[rows:, :] = coef
    losses[...] = loss_zero[...] + loss
    part_one[...] = jnp.dot(coef, everything, preferred_element_type=F32).astype(BF16)


def image_part(coefs, text_units, coef_two, unit_two, place):
    rows = unit_two.shape[0]
    part = slice(place * rows, (place + 1) * rows)
    return by_image(coefs[:, part], text_units[...]) + by_image(coef_two[:, part], unit_two)


def far_kernel(knobs, units, text_units, coefs, losses, texts_two, coef_out, unit_out, loss_out, to_core_top, to_core_low):
    rows, width = texts_two.shape
    unit_two = unit_rows(texts_two[...])[0]
    loss, coef = pair_terms(unit_two, units[...], knobs[0:1, :], knobs[1:2, :])
    unit_out[...] = unit_two
    coef_out[...] = coef
    loss = losses[...] + loss
    loss_out[...] = loss
    part = image_part(coefs, text_units, coef, unit_two, 3).astype(BF16)
    half = rows // 2
    to_core_top[...] = part[:half]
    to_core_low[:half, :] = part[half:]
    to_core_low[half : half + LOSS_ROWS, :] = coded_loss(loss[:, 3 * rows :], width)
    to_core_low[half + LOSS_ROWS :, :] = coded_loss(loss[:, rows : 2 * rows], width)


def rest_kernel(units, text_units, coefs, unit_two, coef_two, to_core, kept, part_two):
    unit = unit_two[...]
    coef = coef_two[...]
    kept[1] = image_part(coefs, text_units, coef, unit, 2)
    kept[0] = image_part(coefs, text_units, coef, unit, 0)
    to_core[...] = image_part(coefs, text_units, coef, unit, 1).astype(BF16)
    part_two[...] = jnp.dot(coef, units[...], preferred_element_type=F32)


def pair_kernel(kept, losses, from_top, from_low, to_across, loss_across):
    rows = kept.shape[1]
    half = rows // 2
    to_across[:half, :] = (kept[1, :half] + from_top[...].astype(F32)).astype(BF16)
    to_across[half:, :] = (kept[1, half:] + from_low[:half, :].astype(F32)).astype(BF16)
    loss_across[...] = losses[:, 2 * rows : 3 * rows] + decoded_loss(from_low[half : half + LOSS_ROWS, :], rows)


def last_kernel(from_across, from_core, loss_across, from_low, units, inverses, kept, losses, text_total, image_grad, row_loss, text_grad):
    rows = image_grad.shape[0]
    grad = kept[0] + from_core[...].astype(F32) + from_across[...].astype(F32)
    wide = units[:rows, :].astype(F32)
    along = jnp.sum(wide * grad, axis=1, keepdims=True)
    image_grad[...] = inverses[:, 0:1] * (grad - wide * along)
    loss = losses[:, :rows] + loss_across[...] + decoded_loss(from_low[rows // 2 + LOSS_ROWS :, :], rows)
    row_loss[...] = loss / (STEPS * 4 * rows)
    text_grad[...] = text_total[...]


def text_kernel(part_zero, part_one, part_two, text_total):
    text_total[...] = part_two[...] + part_one[...].astype(F32) + part_zero[...].astype(F32)


def call(kernel, name, outs, arguments, far=0, flops=0, scratch=()):
    in_specs = [pl.BlockSpec(memory_space=pltpu.HBM)] * far
    in_specs += [pl.BlockSpec(memory_space=pltpu.VMEM)] * (len(arguments) - far)
    moved = sum(a.size * a.dtype.itemsize for a in (*arguments, *outs))
    return pl.pallas_call(
        kernel,
        name=name,
        out_shape=outs,
        in_specs=in_specs,
        out_specs=tuple(pl.BlockSpec(memory_space=pltpu.VMEM) for _ in outs),
        scratch_shapes=scratch,
        cost_estimate=pl.CostEstimate(flops=flops, bytes_accessed=moved, transcendentals=0),
        compiler_params=pltpu.CompilerParams(vmem_limit_bytes=24 * 1024 * 1024),
    )(*arguments)


def shards(images, texts, log_scale, bias):
    rows, width = images.shape
    span = rows * lax.axis_size("grp")
    half = lax.axis_size("blk") // 2
    first_flips = (half - 2,)
    second_flips = (half - 1,)
    made = jax.ShapeDtypeStruct
    texts_one = passed_along(texts, first_flips)
    across = swapped(images, 2)
    core = swapped(images, 1)
    texts_two = passed_two(texts)
    pair = jnp.stack([jnp.exp(log_scale), bias])
    knobs = jnp.broadcast_to(pair, (2, span))
    across, knobs = lax.optimization_barrier((across, knobs))
    diagonal = swapped(across, 1)
    matmul = 2 * rows * span * width
    (unit_one,) = call(unit_kernel, "next_units", (made((rows, width), BF16),), (texts_one,), 0, 30 * matmul)
    image_unit, text_unit, inverses = call(
        own_kernel,
        "own_units",
        (made((rows, width), BF16), made((rows, width), BF16), made((rows, 128), F32)),
        (
            pltpu.with_memory_space_constraint(images, pltpu.HBM),
            pltpu.with_memory_space_constraint(texts, pltpu.HBM),
        ),
        2,
        0 * matmul,
        (pltpu.VMEM((rows, width), BF16), pltpu.VMEM((rows, width), BF16), pltpu.SemaphoreType.DMA((2,))),
    )
    units, text_units, coef_zero, loss_zero, part_zero = call(
        same_kernel,
        "same_texts",
        (
            made((span, width), BF16),
            made((2 * rows, width), BF16),
            made((rows, span), BF16),
            made((1, span), F32),
            made((rows, width), BF16),
        ),
        (knobs, image_unit, text_unit, unit_one, core, across, diagonal),
    )
    part_zero = passed_two(part_zero)
    coefs, losses, part_one = call(
        next_kernel,
        "next_texts",
        (made((2 * rows, span), BF16), made((1, span), F32), made((rows, width), BF16)),
        (knobs, units, text_units, coef_zero, loss_zero),
    )
    part_one = passed_along(part_one, second_flips)
    coef_two, unit_two, losses, to_core_top, to_core_low = call(
        far_kernel,
        "far_texts",
        (
            made((rows, span), BF16),
            made((rows, width), BF16),
            made((1, span), F32),
            made((rows // 2, width), BF16),
            made((rows // 2 + 2 * LOSS_ROWS, width), BF16),
        ),
        (knobs, units, text_units, coefs, losses, texts_two),
    )
    from_core_top = swapped(to_core_top, 1)
    from_core_low = swapped(to_core_low, 1)
    to_core_near, kept, part_two = call(
        rest_kernel,
        "image_parts",
        (made((rows, width), BF16), made((2, rows, width), F32), made((rows, width), F32)),
        (units, text_units, coefs, unit_two, coef_two),
    )
    to_across, loss_across = call(
        pair_kernel,
        "chip_sum",
        (made((rows, width), BF16), made((1, rows), F32)),
        (kept, losses, from_core_top, from_core_low),
    )
    to_across, to_core_near = lax.optimization_barrier((to_across, to_core_near))
    from_across = swapped(to_across, 2)
    from_core_near = swapped(to_core_near, 1)
    loss_across = swapped(loss_across, 2)
    (text_total,) = call(text_kernel, "text_sum", (made((rows, width), F32),), (part_zero, part_one, part_two), 0, 20 * matmul)
    image_grad, row_loss, text_grad = call(
        last_kernel,
        "image_grad",
        (made((rows, width), F32), made((1, rows), F32), made((rows, width), F32)),
        (from_across, from_core_near, loss_across, from_core_low, units, inverses, kept, losses, text_total),
    )
    return (row_loss.reshape(rows), image_grad, text_grad)


def solution(mesh):
    return jax.shard_map(
        shards,
        mesh=mesh,
        in_specs=(P(("blk", "grp"), None), P(("blk", "grp"), None), P(), P()),
        out_specs=(P(("blk", "grp")), P(("blk", "grp"), None), P(("blk", "grp"), None)),
        check_vma=False,
    )
```

```python
import jax
import jax.numpy as jnp
from jax import lax
from jax.experimental import pallas as pl
from jax.experimental.pallas import tpu as pltpu
from jax.sharding import PartitionSpec as P

STEPS = 3
LOSS_ROWS = 16
F32 = jnp.float32
BF16 = jnp.bfloat16


def passed_along(block, flips):
    groups = lax.axis_size("blk")
    members = lax.axis_size("grp")
    route = []
    for group in range(groups):
        flip = 2 if group % (groups // 2) in flips else 0
        for member in range(members):
            target = (group + 1) % groups * members + (member ^ flip)
            route.append((group * members + member, target))
    return lax.ppermute(block, ("blk", "grp"), route)


def passed_two(block):
    groups = lax.axis_size("blk")
    return lax.ppermute(block, "blk", [(i, (i + 2) % groups) for i in range(groups)])


def swapped(block, flip):
    return lax.ppermute(block, "grp", [(i, i ^ flip) for i in range(lax.axis_size("grp"))])


def unit_rows(values):
    wide = values.astype(F32)
    inverse = lax.rsqrt(jnp.sum(wide * wide, axis=-1, keepdims=True) + 1e-06)
    return ((wide * inverse).astype(BF16), inverse)


def pair_terms(text_unit, image_units, scale, bias, positive=None):
    dots = lax.dot_general(
        text_unit, image_units, (((1,), (1,)), ((), ())), preferred_element_type=F32
    )
    logit = scale * dots + bias
    value = logit if positive is None else jnp.where(positive, -logit, logit)
    small = jnp.exp(-jnp.abs(value))
    term = jnp.maximum(value, 0.0) + jnp.log1p(small)
    share = jnp.where(value >= 0.0, 1.0, small) / (1.0 + small)
    coef = share * (scale / STEPS)
    if positive is not None:
        coef = jnp.where(positive, -coef, coef)
    return (jnp.sum(term, axis=0, keepdims=True), coef.astype(BF16))


def by_image(coef, text_unit):
    return lax.dot_general(
        coef, text_unit, (((0,), (0,)), ((), ())), preferred_element_type=F32
    )


def coded_loss(loss, width):
    high = loss.astype(BF16)
    low = (loss - high.astype(F32)).astype(BF16)
    rows = loss.shape[1]
    half = LOSS_ROWS // 2
    parts = [jnp.broadcast_to(part.astype(F32), (half, rows)) for part in (high, low)]
    filled = jnp.concatenate([jnp.concatenate(parts, axis=0), jnp.zeros((LOSS_ROWS, width - rows), F32)], axis=1)
    return filled.astype(BF16)


def decoded_loss(tail, rows):
    wide = tail.astype(F32)
    half = LOSS_ROWS // 2
    return wide[0:1, :rows] + wide[half : half + 1, :rows]


def unit_kernel(texts, text_unit):
    text_unit[...] = unit_rows(texts[...])[0]


def own_kernel(images, texts, image_unit, text_unit, inverses, own_images, own_texts, sems):
    copies = [
        pltpu.make_async_copy(images, own_images, sems.at[0]),
        pltpu.make_async_copy(texts, own_texts, sems.at[1]),
    ]
    for copy in copies:
        copy.start()
    for copy in copies:
        copy.wait()
    unit, inverse = unit_rows(own_images[...])
    image_unit[...] = unit
    inverses[...] = jnp.broadcast_to(inverse, inverses.shape)
    text_unit[...] = unit_rows(own_texts[...])[0]


def same_kernel(knobs, image_unit, text_unit, unit_one, core, across, diagonal, units, text_units, coef_out, losses, part_zero):
    rows = image_unit.shape[0]
    units[:rows, :] = image_unit[...]
    for place, block in ((1, core), (2, across), (3, diagonal)):
        units[place * rows : (place + 1) * rows, :] = unit_rows(block[...])[0]
    unit = text_unit[...]
    text_units[:rows, :] = unit
    text_units[rows:, :] = unit_one[...]
    everything = units[...]
    shape = (rows, everything.shape[0])
    positive = lax.broadcasted_iota(jnp.int32, shape, 0) == lax.broadcasted_iota(jnp.int32, shape, 1)
    loss, coef = pair_terms(unit, everything, knobs[0:1, :], knobs[1:2, :], positive)
    coef_out[...] = coef
    losses[...] = loss
    part_zero[...] = jnp.dot(coef, everything, preferred_element_type=F32).astype(BF16)


def next_kernel(knobs, units, text_units, coef_zero, loss_zero, coefs, losses, part_one):
    rows = coef_zero.shape[0]
    everything = units[...]
    loss, coef = pair_terms(text_units[rows:, :], everything, knobs[0:1, :], knobs[1:2, :])
    coefs[:rows, :] = coef_zero[...]
    coefs[rows:, :] = coef
    losses[...] = loss_zero[...] + loss
    part_one[...] = jnp.dot(coef, everything, preferred_element_type=F32).astype(BF16)


def image_part(coefs, text_units, coef_two, unit_two, place):
    rows = unit_two.shape[0]
    part = slice(place * rows, (place + 1) * rows)
    return by_image(coefs[:, part], text_units[...]) + by_image(coef_two[:, part], unit_two)


def far_kernel(knobs, units, text_units, coefs, losses, texts_two, coef_out, unit_out, loss_out, to_core_top, to_core_low):
    rows, width = texts_two.shape
    unit_two = unit_rows(texts_two[...])[0]
    loss, coef = pair_terms(unit_two, units[...], knobs[0:1, :], knobs[1:2, :])
    unit_out[...] = unit_two
    coef_out[...] = coef
    loss = losses[...] + loss
    loss_out[...] = loss
    part = image_part(coefs, text_units, coef, unit_two, 3).astype(BF16)
    half = rows // 2
    to_core_top[...] = part[:half]
    to_core_low[:half, :] = part[half:]
    to_core_low[half : half + LOSS_ROWS, :] = coded_loss(loss[:, 3 * rows :], width)
    to_core_low[half + LOSS_ROWS :, :] = coded_loss(loss[:, rows : 2 * rows], width)


def rest_kernel(units, text_units, coefs, unit_two, coef_two, to_core, kept, part_two):
    unit = unit_two[...]
    coef = coef_two[...]
    kept[1] = image_part(coefs, text_units, coef, unit, 2)
    kept[0] = image_part(coefs, text_units, coef, unit, 0)
    to_core[...] = image_part(coefs, text_units, coef, unit, 1).astype(BF16)
    part_two[...] = jnp.dot(coef, units[...], preferred_element_type=F32)


def pair_kernel(kept, losses, from_top, from_low, to_across, loss_across):
    rows = kept.shape[1]
    half = rows // 2
    to_across[:half, :] = (kept[1, :half] + from_top[...].astype(F32)).astype(BF16)
    to_across[half:, :] = (kept[1, half:] + from_low[:half, :].astype(F32)).astype(BF16)
    loss_across[...] = losses[:, 2 * rows : 3 * rows] + decoded_loss(from_low[half : half + LOSS_ROWS, :], rows)


def last_kernel(from_across, from_core, loss_across, from_low, units, inverses, kept, losses, text_total, image_grad, row_loss, text_grad, held, sems):
    rows = held.shape[0]
    half = rows // 2
    copies = [pltpu.make_async_copy(text_total, text_grad, sems.at[0])]
    copies[0].start()
    for i in range(2):
        part = slice(i * half, (i + 1) * half)
        grad = kept[0, part] + from_core[part, :].astype(F32) + from_across[part, :].astype(F32)
        wide = units[part, :].astype(F32)
        along = jnp.sum(wide * grad, axis=1, keepdims=True)
        held[part, :] = inverses[part, 0:1] * (grad - wide * along)
        copies.append(pltpu.make_async_copy(held.at[part], image_grad.at[part], sems.at[i + 1]))
        copies[-1].start()
    loss = losses[:, :rows] + loss_across[...] + decoded_loss(from_low[rows // 2 + LOSS_ROWS :, :], rows)
    row_loss[...] = loss / (STEPS * 4 * rows)
    for copy in copies:
        copy.wait()


def text_kernel(part_zero, part_one, part_two, text_total):
    text_total[...] = part_two[...] + part_one[...].astype(F32) + part_zero[...].astype(F32)


def call(kernel, name, outs, arguments, far=0, flops=0, scratch=(), spaces=None):
    in_specs = [pl.BlockSpec(memory_space=pltpu.HBM)] * far
    in_specs += [pl.BlockSpec(memory_space=pltpu.VMEM)] * (len(arguments) - far)
    moved = sum(a.size * a.dtype.itemsize for a in (*arguments, *outs))
    return pl.pallas_call(
        kernel,
        name=name,
        out_shape=outs,
        in_specs=in_specs,
        out_specs=tuple(pl.BlockSpec(memory_space=space) for space in spaces or (pltpu.VMEM,) * len(outs)),
        scratch_shapes=scratch,
        cost_estimate=pl.CostEstimate(flops=flops, bytes_accessed=moved, transcendentals=0),
        compiler_params=pltpu.CompilerParams(vmem_limit_bytes=24 * 1024 * 1024),
    )(*arguments)


def shards(images, texts, log_scale, bias):
    rows, width = images.shape
    span = rows * lax.axis_size("grp")
    half = lax.axis_size("blk") // 2
    first_flips = (half - 2,)
    second_flips = (half - 1,)
    made = jax.ShapeDtypeStruct
    texts_one = passed_along(texts, first_flips)
    across = swapped(images, 2)
    core = swapped(images, 1)
    texts_two = passed_two(texts)
    pair = jnp.stack([jnp.exp(log_scale), bias])
    knobs = jnp.broadcast_to(pair, (2, span))
    across, knobs = lax.optimization_barrier((across, knobs))
    diagonal = swapped(across, 1)
    matmul = 2 * rows * span * width
    (unit_one,) = call(unit_kernel, "next_units", (made((rows, width), BF16),), (texts_one,), 0, 30 * matmul)
    image_unit, text_unit, inverses = call(
        own_kernel,
        "own_units",
        (made((rows, width), BF16), made((rows, width), BF16), made((rows, 128), F32)),
        (
            pltpu.with_memory_space_constraint(images, pltpu.HBM),
            pltpu.with_memory_space_constraint(texts, pltpu.HBM),
        ),
        2,
        0 * matmul,
        (pltpu.VMEM((rows, width), BF16), pltpu.VMEM((rows, width), BF16), pltpu.SemaphoreType.DMA((2,))),
    )
    units, text_units, coef_zero, loss_zero, part_zero = call(
        same_kernel,
        "same_texts",
        (
            made((span, width), BF16),
            made((2 * rows, width), BF16),
            made((rows, span), BF16),
            made((1, span), F32),
            made((rows, width), BF16),
        ),
        (knobs, image_unit, text_unit, unit_one, core, across, diagonal),
    )
    part_zero = passed_two(part_zero)
    coefs, losses, part_one = call(
        next_kernel,
        "next_texts",
        (made((2 * rows, span), BF16), made((1, span), F32), made((rows, width), BF16)),
        (knobs, units, text_units, coef_zero, loss_zero),
    )
    part_one = passed_along(part_one, second_flips)
    coef_two, unit_two, losses, to_core_top, to_core_low = call(
        far_kernel,
        "far_texts",
        (
            made((rows, span), BF16),
            made((rows, width), BF16),
            made((1, span), F32),
            made((rows // 2, width), BF16),
            made((rows // 2 + 2 * LOSS_ROWS, width), BF16),
        ),
        (knobs, units, text_units, coefs, losses, texts_two),
    )
    from_core_top = swapped(to_core_top, 1)
    from_core_low = swapped(to_core_low, 1)
    to_core_near, kept, part_two = call(
        rest_kernel,
        "image_parts",
        (made((rows, width), BF16), made((2, rows, width), F32), made((rows, width), F32)),
        (units, text_units, coefs, unit_two, coef_two),
    )
    to_across, loss_across = call(
        pair_kernel,
        "chip_sum",
        (made((rows, width), BF16), made((1, rows), F32)),
        (kept, losses, from_core_top, from_core_low),
    )
    to_across, to_core_near = lax.optimization_barrier((to_across, to_core_near))
    from_across = swapped(to_across, 2)
    from_core_near = swapped(to_core_near, 1)
    loss_across = swapped(loss_across, 2)
    (text_total,) = call(text_kernel, "text_sum", (made((rows, width), F32),), (part_zero, part_one, part_two), 0, 20 * matmul)
    image_grad, row_loss, text_grad = call(
        last_kernel,
        "image_grad",
        (made((rows, width), F32), made((1, rows), F32), made((rows, width), F32)),
        (from_across, from_core_near, loss_across, from_core_low, units, inverses, kept, losses, text_total),
        0,
        0,
        (pltpu.VMEM((rows, width), F32), pltpu.SemaphoreType.DMA((3,))),
        (pltpu.HBM, pltpu.VMEM, pltpu.HBM),
    )
    return (row_loss.reshape(rows), image_grad, text_grad)


def solution(mesh):
    return jax.shard_map(
        shards,
        mesh=mesh,
        in_specs=(P(("blk", "grp"), None), P(("blk", "grp"), None), P(), P()),
        out_specs=(P(("blk", "grp")), P(("blk", "grp"), None), P(("blk", "grp"), None)),
        check_vma=False,
    )
```
